128 devices in a mesh: group: 32 (over y, z, core), tp: 4 (over x).
Axes of the slice: x: 4, y: 4, z: 4, core: 2. Of those that a mesh axis runs over, the one named last changes fastest.
Arguments:
- queries: bfloat16 [5120, 6144], P('group', 'tp'), may hold values from -180 to 180
- keys: bfloat16 [5120, 6144], P('group', 'tp'), may hold values from -6.2 to 6.2
- values: bfloat16 [5120, 6144], P('group', 'tp'), may hold values from -24 to 24
- out_weight: bfloat16 [6144, 6144], P('tp'), may hold values from -0.078125 to 0.078125
- gate_table: float32 [16, 6144], replicated, may hold values from 0.5 to 4
- block_mask: int32 [32, 32], replicated, may hold values 0 or 1
- levels: int32 [4], replicated, may hold values from 0 to 15
Outputs:
- update: bfloat16 [5120, 6144], P('group', 'tp')
The draws below stay inside these ranges and needn't reach their ends.
All inputs are finite; a program needn't handle non-finite values.
Results may differ from the reference program's by a relative error of at most 0.017.
Values may be sent and summed in bfloat16 or wider, within the bound.
No kernel may reach another device: no remote copies, remote signals or barrier semaphores. Data moves between devices by JAX's collectives and lax.ppermute only.
A program may use at most 128 MiB of HBM per device.

```python
import math
import jax
import jax.numpy as jnp
from jax import lax

D = 6144
HEADS = 48
HEAD_DIM = 128
VIDEO_GROUPS = 4
LEVELS = 16
TOK_DEV = 160
BLOCKS = 32
TOKENS = 5120


def shared_keys(key):
    return jnp.clip(jax.random.normal(key, (TOKENS, HEADS * HEAD_DIM), jnp.float32), -6.0, 6.0)


def draw_keys(key, part):
    base_keys = shared_keys(key)
    return base_keys.astype(jnp.bfloat16)


def draw_queries(key, part):
    key = jax.random.fold_in(key, 12)
    fresh = jnp.clip(2.0 * jax.random.normal(key, (TOKENS, HEADS * HEAD_DIM), jnp.float32), -12.0, 12.0)
    return fresh.astype(jnp.bfloat16)


def set_ends(entries, stream_key, low, top_value):
    shape = entries.shape
    place = [jax.random.randint(jax.random.fold_in(stream_key, axis), (), 0, shape[axis]) for axis in range(len(shape))]
    entries = entries.at[tuple(place)].set(low)
    longest = shape.index(max(shape))
    place[longest] = (place[longest] + 1) % shape[longest]
    return entries.at[tuple(place)].set(top_value)


def steps_of(own_key, extent, shards, low, top_value):
    def one(dim, shards_of):
        heights = jax.random.uniform(jax.random.fold_in(jax.random.fold_in(own_key, 6), dim), (shards_of,), jnp.float32, low / len(shards), top_value / len(shards))
        return jnp.repeat(jnp.exp(heights), extent[dim] // shards_of).reshape((-1,) + (1,) * (len(extent) - dim - 1))

    gain = one(*shards[0])
    for cut in shards[1:]:
        gain = gain * one(*cut)
    return gain


def noise(rng, dims, scale, reach, pieces=(), kind=jnp.bfloat16):
    drawn = jax.random.normal(rng, dims, jnp.float32) * scale
    if len(pieces) > 0:
        drawn = steps_of(rng, dims, pieces, -0.22, 0.18) * drawn
    return jnp.clip(drawn, min=-reach, max=reach).astype(kind)


def setup_inputs(seed: int = 0) -> dict:
    key_list = jax.random.split(jax.random.key(seed), 8)
    return {
        "queries": draw_queries(jax.random.fold_in(key_list[7], 71), 0),
        "keys": draw_keys(jax.random.fold_in(key_list[7], 71), 0),
        "values": noise(key_list[2], (TOKENS, HEADS * HEAD_DIM), 4.0, 24.0, ((0, 32), (1, 4))),
        "out_weight": noise(key_list[3], (HEADS * HEAD_DIM, D), (HEADS * HEAD_DIM) ** -0.5, 0.078125, ((0, 4),)),
        "gate_table": jnp.clip(jnp.exp(jax.random.uniform(key_list[4], (LEVELS, D), jnp.float32, math.log(0.5), math.log(4.0))), 0.5, 4.0),
        "block_mask": set_ends((jax.random.randint(key_list[5], (BLOCKS, BLOCKS), 0, 4) < 3).astype(jnp.int32), jax.random.fold_in(key_list[5], 1), 0, 1),
        "levels": set_ends(jax.random.randint(key_list[6], (VIDEO_GROUPS,), 0, LEVELS), jax.random.fold_in(key_list[6], 1), 0, LEVELS - 1).astype(jnp.int32),
    }


masked_score = -1e30


def visible_blocks(block_mask, query_block, block_count):
    key_block = jnp.arange(block_count, dtype=jnp.int32)
    per_group = block_count // VIDEO_GROUPS
    mask_row = jnp.sum(jnp.where(key_block[:, None] == query_block, block_mask, 0), axis=0)
    earlier = key_block // per_group <= query_block // per_group
    return (key_block == query_block) | ((mask_row == 1) & earlier)


def absorb_block(state, query_rows, key_rows, value_rows):
    running_max, running_sum, running_out = state
    scores = jnp.einsum("qhd,khd->hqk", query_rows.astype(jnp.float32), key_rows.astype(jnp.float32)) * (HEAD_DIM ** -0.5)
    block_max = jnp.max(scores, axis=-1)
    weights = jnp.exp(scores - block_max[..., None]).astype(jnp.bfloat16)
    block_sum = jnp.sum(weights.astype(jnp.float32), axis=-1)
    block_out = jnp.einsum("hqk,khd->hqd", weights.astype(jnp.float32), value_rows.astype(jnp.float32))
    new_max = jnp.maximum(running_max, block_max)
    old_factor = jnp.exp(running_max - new_max)
    new_factor = jnp.exp(block_max - new_max)
    return (new_max, running_sum * old_factor + block_sum * new_factor,
            running_out * old_factor[..., None] + block_out * new_factor[..., None])


def reference(queries, keys, values, out_weight, gate_table, block_mask, levels):
    key_blocks = keys.reshape(BLOCKS, TOK_DEV, HEADS, HEAD_DIM)
    value_blocks = values.reshape(BLOCKS, TOK_DEV, HEADS, HEAD_DIM)

    def attend_block(query_block):
        query_rows = lax.dynamic_slice_in_dim(queries, query_block * TOK_DEV, TOK_DEV, 0).reshape(TOK_DEV, HEADS, HEAD_DIM)
        visible = visible_blocks(block_mask, query_block, BLOCKS)
        start_state = (jnp.full((HEADS, TOK_DEV), masked_score, jnp.float32),
                       jnp.zeros((HEADS, TOK_DEV), jnp.float32),
                       jnp.zeros((HEADS, TOK_DEV, HEAD_DIM), jnp.float32))

        def visit(state, inputs):
            key_rows, value_rows, seen = inputs
            updated = absorb_block(state, query_rows, key_rows, value_rows)
            kept = jax.tree.map(lambda after, before: jnp.where(seen, after, before), updated, state)
            return kept, None

        final_state, ignored = lax.scan(visit, start_state, (key_blocks, value_blocks, visible))
        normed = final_state[2] / final_state[1][..., None]
        return jnp.transpose(normed, (1, 0, 2)).reshape(TOK_DEV, HEADS * HEAD_DIM).astype(jnp.bfloat16)

    attended = lax.map(attend_block, jnp.arange(BLOCKS, dtype=jnp.int32))
    projected = jnp.dot(attended.reshape(TOKENS, HEADS * HEAD_DIM), out_weight, preferred_element_type=jnp.float32)
    projected = projected.reshape(BLOCKS, TOK_DEV, D)
    group_of = jnp.arange(BLOCKS, dtype=jnp.int32) // (BLOCKS // VIDEO_GROUPS)
    level_of = levels[group_of]
    gates = gate_table[level_of]
    update = (projected * gates[:, None, :]).reshape(TOKENS, D).astype(jnp.bfloat16)
    return update
```

```python
import functools

import jax
import jax.numpy as jnp
from jax import lax
from jax.experimental import pallas as pl
from jax.experimental.pallas import tpu as pltpu
from jax.sharding import Mesh, PartitionSpec as P

HEAD_DIM = 128
VIDEO_GROUPS = 4
TOK = 160
LOG2E = 1.4426950408889634

masked_score = -1e30


def visible_matrix(block_mask):
    blocks = block_mask.shape[0]
    block = jnp.arange(blocks, dtype=jnp.int32)
    per_group = blocks // VIDEO_GROUPS
    earlier = block[None, :] // per_group <= block[:, None] // per_group
    return (block[None, :] == block[:, None]) | ((block_mask == 1) & earlier)


def attend_kernel(pieces, bias_ref, q_ref, k_ref, v_ref, o_ref):
    factor = HEAD_DIM ** -0.5 * LOG2E
    for yq in range(VIDEO_GROUPS):
        n = TOK * (yq + 1)
        q = q_ref[yq]
        scores = []
        for p in range(pieces):
            s = lax.dot_general(
                q, k_ref[p, :n, :], (((1,), (1,)), ((), ())), preferred_element_type=jnp.float32
            )
            scores.append(s + bias_ref[p, yq : yq + 1, :n])
        top = functools.reduce(jnp.maximum, [jnp.max(s, axis=-1, keepdims=True) for s in scores])
        total = jnp.zeros((q.shape[0], 2 * HEAD_DIM), jnp.float32)
        for p in range(pieces):
            weights = jnp.exp2((scores[p] - top) * factor).astype(jnp.bfloat16)
            values = jnp.concatenate(
                [v_ref[p, :n, :], jnp.ones((n, HEAD_DIM), jnp.bfloat16)], axis=1
            )
            total = total + jnp.dot(weights, values, preferred_element_type=jnp.float32)
        o_ref[yq] = (total[:, :HEAD_DIM] / total[:, HEAD_DIM:]).astype(o_ref.dtype)


def attend(bias, q, kv):
    pieces, keys_here = kv.shape[:2]
    rows = q.shape[1]
    heads = q.shape[2] // HEAD_DIM
    return pl.pallas_call(
        functools.partial(attend_kernel, pieces),
        grid=(heads,),
        in_specs=[
            pl.BlockSpec(bias.shape, lambda h: (0, 0, 0)),
            pl.BlockSpec((VIDEO_GROUPS, rows, HEAD_DIM), lambda h: (0, 0, h)),
            pl.BlockSpec((pieces, keys_here, HEAD_DIM), lambda h: (0, 0, h)),
            pl.BlockSpec((pieces, keys_here, HEAD_DIM), lambda h: (0, 0, heads + h)),
        ],
        out_specs=pl.BlockSpec((VIDEO_GROUPS, rows, HEAD_DIM), lambda h: (0, 0, h)),
        out_shape=jax.ShapeDtypeStruct(q.shape, jnp.bfloat16),
        compiler_params=pltpu.CompilerParams(vmem_limit_bytes=48 * 2**20),
    )(bias, q, kv, kv)


def local(queries, keys, values, out_weight, gate_table, block_mask, levels):
    y, z, core = lax.axis_index("y"), lax.axis_index("z"), lax.axis_index("core")
    own = z * 2 + core
    visible = visible_matrix(block_mask).reshape(4, 8, 4, 8)
    seen = lax.dynamic_index_in_dim(visible, own, 1, keepdims=False)
    bias = jnp.where(jnp.transpose(seen, (2, 0, 1)), 0.0, masked_score).astype(jnp.float32)
    bias = jnp.repeat(bias, TOK, axis=2)

    parts = jnp.concatenate([a.reshape(TOK, 4, -1) for a in (queries, keys, values)], axis=2)
    width = queries.shape[1] // 4
    swapped = lax.all_to_all(jnp.transpose(parts, (1, 0, 2)), "y", 0, 0, tiled=True)
    q = swapped[:, :, :width]
    kv = swapped[:, :, width:].reshape(1, 4 * TOK, 2 * width)
    kv = lax.all_gather(kv, ("z", "core"), axis=0, tiled=True)
    out = attend(bias, q, kv)
    attended = lax.all_to_all(out, "y", 0, 0, tiled=True)
    attended = jnp.transpose(attended, (1, 0, 2)).reshape(TOK, -1)

    head_terms = jnp.dot(attended, out_weight, preferred_element_type=jnp.float32)
    summed = lax.psum_scatter(
        head_terms.astype(jnp.bfloat16), "tp", scatter_dimension=1, tiled=True
    ).astype(jnp.float32)
    columns = summed.shape[1]
    gate_part = lax.dynamic_slice(
        gate_table,
        (lax.dynamic_index_in_dim(levels, y, keepdims=False), lax.axis_index("tp") * columns),
        (1, columns),
    )
    return (summed * gate_part).astype(jnp.bfloat16)


def solution(mesh):
    fine = Mesh(mesh.devices.reshape(4, 4, 2, 4), ("y", "z", "core", "tp"))
    group = ("y", "z", "core")
    return jax.shard_map(
        local,
        mesh=fine,
        in_specs=(
            P(group, "tp"),
            P(group, "tp"),
            P(group, "tp"),
            P("tp", None),
            P(),
            P(),
            P(),
        ),
        out_specs=P(group, "tp"),
        check_vma=False,
    )
```

```python
import functools

import jax
import jax.numpy as jnp
from jax import lax
from jax.experimental import pallas as pl
from jax.experimental.pallas import tpu as pltpu
from jax.sharding import Mesh, PartitionSpec as P

HEAD_DIM = 128
VIDEO_GROUPS = 4
TOK = 160
HEADS = 3
WIDTH = HEADS * HEAD_DIM
FACTOR = HEAD_DIM ** -0.5 * 1.4426950408889634

masked_score = -1e30
VMEM_GRANT = 56 * 2**20
VMEM_SMALL = 8 * 2**20


def visible_matrix(block_mask):
    blocks = block_mask.shape[0]
    block = jnp.arange(blocks, dtype=jnp.int32)
    per_group = blocks // VIDEO_GROUPS
    earlier = block[None, :] // per_group <= block[:, None] // per_group
    return (block[None, :] == block[:, None]) | ((block_mask == 1) & earlier)


Y_OFFSETS = (0, 3, 1, 2)


def start_all(copies):
    for copy in copies:
        copy.start()


def wait_all(copies):
    for copy in copies:
        copy.wait()


def pack_kernel(place_ref, queries, keys, values, *refs):
    outs, (both_s, query_s, sems, out_sems) = refs[:-4], refs[-4:]
    arrive, leave = [], []
    for j, distance in enumerate((0, 1, 3, 2)):
        first = lax.rem(place_ref[1] + distance, 4) * WIDTH
        source = pl.ds(pl.multiple_of(first, WIDTH), WIDTH)
        pairs = (
            (keys.at[:, source], both_s.at[j, :, pl.ds(0, WIDTH)]),
            (values.at[:, source], both_s.at[j, :, pl.ds(WIDTH, WIDTH)]),
            (queries.at[:, source], query_s.at[j]),
        )
        for i, (src, dst) in enumerate(pairs):
            arrive.append(pltpu.make_async_copy(src, dst, sems.at[3 * j + i]))
        leave.append(pltpu.make_async_copy(both_s.at[j], outs[j], out_sems.at[j]))
        leave.append(pltpu.make_async_copy(query_s.at[j], outs[4 + j], out_sems.at[4 + j]))
    start_all(arrive)
    for j in range(4):
        wait_all(arrive[3 * j : 3 * j + 3])
        start_all(leave[2 * j : 2 * j + 2])
    wait_all(leave)


def pack_by_owner(place, queries, keys, values):
    shape = lambda width: jax.ShapeDtypeStruct((TOK, width), jnp.bfloat16)
    hbm = pl.BlockSpec(memory_space=pltpu.HBM)
    outs = pl.pallas_call(
        pack_kernel,
        in_specs=[pl.BlockSpec(memory_space=pltpu.SMEM), hbm, hbm, hbm],
        out_specs=[hbm] * 8,
        out_shape=[shape(2 * WIDTH)] * 4 + [shape(WIDTH)] * 4,
        scratch_shapes=[
            pltpu.VMEM((4, TOK, 2 * WIDTH), jnp.bfloat16),
            pltpu.VMEM((4, TOK, WIDTH), jnp.bfloat16),
            pltpu.SemaphoreType.DMA((12,)),
            pltpu.SemaphoreType.DMA((8,)),
        ],
        compiler_params=pltpu.CompilerParams(vmem_limit_bytes=VMEM_GRANT),
        name="pack_by_owner",
    )(place, queries, keys, values)
    return outs[:4], outs[4:]


def stack_kernel(*refs):
    parts, out, sems = refs[:-2], refs[-2], refs[-1]
    rows = parts[0].shape[0]
    copies = [
        pltpu.make_async_copy(part, out.at[pl.ds(i * rows, rows), :], sems.at[i])
        for i, part in enumerate(parts)
    ]
    start_all(copies)
    wait_all(copies)


def stack(*parts):
    rows, width = parts[0].shape
    return pl.pallas_call(
        stack_kernel,
        in_specs=[pl.BlockSpec(memory_space=pltpu.VMEM)] * len(parts),
        out_specs=pl.BlockSpec(memory_space=pltpu.HBM),
        out_shape=jax.ShapeDtypeStruct((len(parts) * rows, width), parts[0].dtype),
        scratch_shapes=[pltpu.SemaphoreType.DMA((len(parts),))],
        compiler_params=pltpu.CompilerParams(vmem_limit_bytes=VMEM_SMALL),
        name="stack",
    )(*parts)


def take_kernel(first, x_ref, o_ref, sem):
    rows = o_ref.shape[0]
    copy = pltpu.make_async_copy(x_ref.at[pl.ds(first, rows), :], o_ref, sem)
    copy.start()
    copy.wait()


def take_rows(x, first, rows):
    return pl.pallas_call(
        functools.partial(take_kernel, first),
        in_specs=[pl.BlockSpec(memory_space=pltpu.VMEM)],
        out_specs=pl.BlockSpec(memory_space=pltpu.HBM),
        out_shape=jax.ShapeDtypeStruct((rows, x.shape[1]), x.dtype),
        scratch_shapes=[pltpu.SemaphoreType.DMA],
        compiler_params=pltpu.CompilerParams(vmem_limit_bytes=VMEM_SMALL),
        name="take_rows",
    )(x)


FIRST_SEGMENTS = ((0, 0, 160, 0, 0), (1, 0, 160, 1, 0), (1, 160, 160, 2, 0), (1, 320, 160, 3, 0))
FAR_SEGMENTS = (
    (0, 0, 160, 0, 0), (1, 0, 160, 1, 0), (1, 160, 80, 2, 0), (2, 0, 80, 2, 80), (2, 80, 160, 3, 0)
)


def lay_out(y, head, qs, parts, segments, q_s, k_s, v_s):
    arrays = 1 + max(segment[0] for segment in segments)
    pieces = len(parts) // arrays
    keys = slice(head * HEAD_DIM, (head + 1) * HEAD_DIM)
    values = slice((HEADS + head) * HEAD_DIM, (HEADS + head + 1) * HEAD_DIM)
    for j, offset in enumerate(Y_OFFSETS):
        group = lax.rem(y + offset, 4)
        for r in range(2):
            place = pl.ds(pl.multiple_of((group * 2 + r) * TOK, TOK), TOK)
            q_s[head, place, :] = qs[r][j * TOK : (j + 1) * TOK, keys]
    for array, row, rows, j, start in segments:
        group = lax.rem(y + Y_OFFSETS[j], 4)
        for p in range(pieces):
            part = parts[arrays * p + array]
            place = pl.ds(pl.multiple_of((group * pieces + p) * TOK + start, 16), rows)
            k_s[head, place, :] = part[row : row + rows, keys]
            v_s[head, place, :HEAD_DIM] = part[row : row + rows, values]
    v_s[head, :, HEAD_DIM:] = jnp.ones((v_s.shape[1], HEAD_DIM), jnp.bfloat16)


def partial_attention(bias_ref, q_s, k_s, v_s, head, yq):
    n = k_s.shape[1] // 4 * (yq + 1)
    q = q_s[head, 2 * TOK * yq : 2 * TOK * (yq + 1), :]
    s = lax.dot_general(
        q, k_s[head, :n, :], (((1,), (1,)), ((), ())), preferred_element_type=jnp.float32
    )
    s = s + jnp.concatenate(
        [jnp.broadcast_to(bias_ref[r, yq : yq + 1, :n], (TOK, n)) for r in range(2)], axis=0
    )
    top = jnp.max(s, axis=-1, keepdims=True)
    weights = jnp.exp2((s - top) * FACTOR).astype(jnp.bfloat16)
    return top, jnp.dot(weights, v_s[head, :n, :], preferred_element_type=jnp.float32)


def first_kernel(place_ref, bias_ref, *refs):
    qs, parts, (o_ref, lse_ref), scratch = refs[:2], refs[2:-5], refs[-5:-3], refs[-3:]
    for head in range(HEADS):
        columns = slice(head * HEAD_DIM, (head + 1) * HEAD_DIM)
        lay_out(place_ref[1], head, qs, parts, FIRST_SEGMENTS, *scratch)
        for yq in range(VIDEO_GROUPS):
            top, total = partial_attention(bias_ref, *scratch, head, yq)
            weight_sum = total[:, HEAD_DIM:]
            o_ref[yq, :, columns] = total[:, :HEAD_DIM] / weight_sum
            lse_ref[yq, :, columns] = top * FACTOR + jnp.log2(weight_sum)


def last_kernel(place_ref, bias_ref, *refs):
    qs, parts, scratch = refs[:2], refs[2:-9], refs[-3:]
    o_in, lse_in, o0, o1, lse0, lse1 = refs[-9:-3]
    for head in range(HEADS):
        columns = slice(head * HEAD_DIM, (head + 1) * HEAD_DIM)
        lay_out(place_ref[1], head, qs, parts, FAR_SEGMENTS, *scratch)
        for yq in range(VIDEO_GROUPS):
            top, total = partial_attention(bias_ref, *scratch, head, yq)
            scaled = top * FACTOR
            before = lse_in[yq, :, columns]
            both = jnp.maximum(scaled, before)
            new_factor = jnp.exp2(scaled - both)
            old_factor = jnp.exp2(before - both)
            weight_sum = total[:, HEAD_DIM:] * new_factor + old_factor
            out = total[:, :HEAD_DIM] * new_factor + o_in[yq, :, columns] * old_factor
            out = (out / weight_sum).astype(jnp.bfloat16)
            lse = both + jnp.log2(weight_sum)
            o0[yq, :, columns], o1[yq, :, columns] = out[:TOK], out[TOK:]
            lse0[yq, :, columns], lse1[yq, :, columns] = lse[:TOK], lse[TOK:]


def attention_call(kernel, place, bias, qs, parts, state, outs, keys_here, name, flops):
    vmem = pl.BlockSpec(memory_space=pltpu.VMEM)
    operands = (bias, *qs, *parts, *state)
    return pl.pallas_call(
        kernel,
        in_specs=[pl.BlockSpec(memory_space=pltpu.SMEM)] + [vmem] * len(operands),
        out_specs=[vmem] * len(outs),
        out_shape=outs,
        scratch_shapes=[
            pltpu.VMEM((HEADS, 8 * TOK, HEAD_DIM), jnp.bfloat16),
            pltpu.VMEM((HEADS, keys_here, HEAD_DIM), jnp.bfloat16),
            pltpu.VMEM((HEADS, keys_here, 2 * HEAD_DIM), jnp.bfloat16),
        ],
        compiler_params=pltpu.CompilerParams(vmem_limit_bytes=20 * 2**20),
        cost_estimate=pl.CostEstimate(flops=flops, bytes_accessed=2**20, transcendentals=0),
        name=name,
    )(place, *operands)


def merge_kernel(place_ref, oa, la, ob, lb, *outs):
    for out_ref, distance in zip(outs, (0, 1, 3, 2)):
        group = lax.rem(place_ref[1] + distance, 4)
        a, b = la[group], lb[group]
        top = jnp.maximum(a, b)
        wa, wb = jnp.exp2(a - top), jnp.exp2(b - top)
        out = oa[group].astype(jnp.float32) * wa + ob[group].astype(jnp.float32) * wb
        out_ref[...] = (out / (wa + wb)).astype(out_ref.dtype)


def merge_cores(place, oa, la, ob, lb):
    vmem = pl.BlockSpec(memory_space=pltpu.VMEM)
    return pl.pallas_call(
        merge_kernel,
        in_specs=[pl.BlockSpec(memory_space=pltpu.SMEM)] + [vmem] * 4,
        out_specs=[vmem] * 4,
        out_shape=[jax.ShapeDtypeStruct((TOK, WIDTH), jnp.bfloat16)] * 4,
        compiler_params=pltpu.CompilerParams(vmem_limit_bytes=VMEM_SMALL),
        name="merge_cores",
    )(place, oa, la, ob, lb)


def project_kernel(places, added, place_ref, *refs):
    parts, w_ref, refs = refs[:4], refs[4], refs[5:]
    extra, outs, rows_s = refs[:added], refs[added:-1], refs[-1]
    for part, offset in zip(parts, Y_OFFSETS):
        first = lax.rem(place_ref[1] + offset, 4) * WIDTH
        rows_s[:, pl.ds(pl.multiple_of(first, WIDTH), WIDTH)] = part[...]
    columns = w_ref.shape[1] // 8
    for i, (distance, half) in enumerate(places):
        first = (lax.rem(place_ref[0] + distance, 4) * 2 + half) * columns
        weights = w_ref[:, pl.ds(pl.multiple_of(first, columns), columns)]
        term = jnp.dot(rows_s[...], weights, preferred_element_type=jnp.float32)
        if added:
            term = term + extra[i][...].astype(jnp.float32)
        outs[i][...] = term.astype(outs[i].dtype)


def project(place, attended, out_weight, places, extra=(), dtype=jnp.bfloat16):
    depth, columns = out_weight.shape[0], out_weight.shape[1] // 8
    count = len(places)
    vmem = pl.BlockSpec(memory_space=pltpu.VMEM)
    return pl.pallas_call(
        functools.partial(project_kernel, places, len(extra)),
        in_specs=[pl.BlockSpec(memory_space=pltpu.SMEM)] + [vmem] * (5 + len(extra)),
        out_specs=[vmem] * count,
        out_shape=[jax.ShapeDtypeStruct((TOK, columns), dtype)] * count,
        scratch_shapes=[pltpu.VMEM((TOK, depth), jnp.bfloat16)],
        compiler_params=pltpu.CompilerParams(vmem_limit_bytes=VMEM_SMALL),
        cost_estimate=pl.CostEstimate(
            flops=2 * count * TOK * depth * columns,
            bytes_accessed=2 * count * depth * columns,
            transcendentals=0,
        ),
        name="project",
    )(place, *attended, out_weight, *extra)


def final_kernel(own_a, own_b, direct_a, direct_b, summed_a, summed_b, gate_ref, o_ref):
    columns = own_a.shape[1]
    for i, (own, direct, summed) in enumerate(
        ((own_a, direct_a, summed_a), (own_b, direct_b, summed_b))
    ):
        place = slice(i * columns, (i + 1) * columns)
        total = own[...] + direct[...].astype(jnp.float32) + summed[...].astype(jnp.float32)
        o_ref[:, place] = (total * gate_ref[:, place]).astype(o_ref.dtype)


def finish(halves, gate):
    rows, columns = halves[0].shape
    vmem = pl.BlockSpec(memory_space=pltpu.VMEM)
    return pl.pallas_call(
        final_kernel,
        in_specs=[vmem] * 7,
        out_specs=vmem,
        out_shape=jax.ShapeDtypeStruct((rows, 2 * columns), jnp.bfloat16),
        compiler_params=pltpu.CompilerParams(vmem_limit_bytes=VMEM_SMALL),
        name="finish",
    )(*halves, gate)


def shift(x, axis, step):
    size = lax.axis_size(axis)
    return lax.ppermute(x, axis, [(i, (i + step) % size) for i in range(size)])


def local(queries, keys, values, out_weight, gate_table, block_mask, levels):
    barrier = lax.optimization_barrier
    x, y, z, core = (lax.axis_index(name) for name in ("tp", "y", "z", "core"))
    place = jnp.stack([x, y, z, core])

    visible = visible_matrix(block_mask).reshape(4, 4, 2, 4, 4, 2)
    seen = lax.dynamic_index_in_dim(visible, z, 1, keepdims=False)
    seen = lax.dynamic_index_in_dim(seen, core, 4, keepdims=False)
    seen = jnp.stack(
        [lax.dynamic_index_in_dim(seen, c, 1, keepdims=False) for c in (core, 1 - core)], axis=0
    )
    seen = jnp.stack(
        [lax.dynamic_index_in_dim(seen, (z + d) % 4, 3, keepdims=False) for d in (0, 3, 1, 2)],
        axis=3,
    )
    bias = jnp.repeat(jnp.where(seen, 0.0, masked_score).astype(jnp.float32), TOK, axis=3)
    bias = bias.reshape(2, 4, 4, 4 * TOK)
    bias_first = bias[..., : 3 * TOK].reshape(2, 4, 12 * TOK)
    bias_last = bias[..., 3 * TOK :].reshape(2, 4, 4 * TOK)

    columns = gate_table.shape[1] // 4
    gate_part = lax.dynamic_slice(
        gate_table,
        (lax.dynamic_index_in_dim(levels, y, keepdims=False), x * columns),
        (1, columns),
    )

    (own, up, down, across), (q_own, q_up, q_down, q_across) = pack_by_owner(
        place, queries, keys, values
    )
    from_down, from_up = shift(up, "y", 1), shift(down, "y", -1)
    from_across = shift(across, "y", 2)
    own_before, own_after = shift(own, "z", 1), shift(own, "z", -1)

    own_far = shift(own_before, "z", 1)

    arrived = (from_down, from_up, from_across, q_up, q_down, q_across)
    arrived, own_before, own_after, own_far, bias_first, bias_last, gate_part = barrier(
        (arrived, own_before, own_after, own_far, bias_first, bias_last, gate_part)
    )
    from_down, from_up, from_across, q_up, q_down, q_across = arrived
    rest = stack(from_down, from_up, from_across)
    rest_before, rest_after = shift(rest, "z", 1), shift(rest, "z", -1)
    q_here = stack(q_own, shift(q_up, "y", 1), shift(q_down, "y", -1), shift(q_across, "y", 2))
    q_there = shift(q_here, "core", 1)
    q_there, rest_before, rest_after = barrier((q_there, rest_before, rest_after))
    half = rest.shape[0] // 2
    far = (
        own_far,
        shift(take_rows(rest_before, 0, half), "z", 1),
        shift(take_rows(rest_after, half, half), "z", -1),
    )
    qs = (q_here, q_there)
    parts = (own, rest, own_before, rest_before, own_after, rest_after)

    both = lambda dtype: jax.ShapeDtypeStruct((VIDEO_GROUPS, 2 * TOK, WIDTH), dtype)
    one = lambda dtype: jax.ShapeDtypeStruct((VIDEO_GROUPS, TOK, WIDTH), dtype)
    f32, bf16 = jnp.float32, jnp.bfloat16
    state = attention_call(
        first_kernel, place, bias_first, qs, parts, (),
        [both(f32), both(f32)], 12 * TOK, "attend_first", 100 * 10**9,
    )
    o_own, o_other, lse_own, lse_other = attention_call(
        last_kernel, place, bias_last, qs, far, state,
        [one(bf16), one(bf16), one(f32), one(f32)], 4 * TOK, "attend_last", 6 * 10**9,
    )
    out, out_up, out_down, out_across = merge_cores(
        place, o_own, lse_own, shift(o_other, "core", 1), shift(lse_other, "core", 1)
    )
    attended = (out, shift(out_up, "y", 1), shift(out_down, "y", -1), shift(out_across, "y", 2))

    across_a, across_b = project(place, attended, out_weight, ((2, 0), (2, 1)))
    from_left, from_right = shift(across_a, "tp", 1), shift(across_b, "tp", -1)
    right_b, left_a = project(place, attended, out_weight, ((1, 1), (3, 0)))
    direct_b, direct_a = shift(right_b, "tp", 1), shift(left_a, "tp", -1)
    own_a, own_b = project(place, attended, out_weight, ((0, 0), (0, 1)), dtype=f32)
    right_a, left_b = project(
        place, attended, out_weight, ((1, 0), (3, 1)), (from_left, from_right)
    )
    summed_a, summed_b = shift(right_a, "tp", 1), shift(left_b, "tp", -1)
    return finish((own_a, own_b, direct_a, direct_b, summed_a, summed_b), gate_part)


def solution(mesh):
    fine = Mesh(mesh.devices.reshape(4, 4, 2, 4), ("y", "z", "core", "tp"))
    group = ("y", "z", "core")
    return jax.shard_map(
        local,
        mesh=fine,
        in_specs=(
            P(group, "tp"),
            P(group, "tp"),
            P(group, "tp"),
            P("tp", None),
            P(),
            P(),
            P(),
        ),
        out_specs=P(group, "tp"),
        check_vma=False,
    )
```

```python
import functools

import jax
import jax.numpy as jnp
from jax import lax
from jax.experimental import pallas as pl
from jax.experimental.pallas import tpu as pltpu
from jax.sharding import Mesh, PartitionSpec as P

HEAD_DIM = 128
VIDEO_GROUPS = 4
TOK = 160
HEADS = 3
WIDTH = HEADS * HEAD_DIM
FACTOR = HEAD_DIM ** -0.5 * 1.4426950408889634

masked_score = -1e30
VMEM_GRANT = 56 * 2**20
VMEM_SMALL = 8 * 2**20
LOG_LANES = 32


def visible_matrix(block_mask):
    blocks = block_mask.shape[0]
    block = jnp.arange(blocks, dtype=jnp.int32)
    per_group = blocks // VIDEO_GROUPS
    earlier = block[None, :] // per_group <= block[:, None] // per_group
    return (block[None, :] == block[:, None]) | ((block_mask == 1) & earlier)


def take_kernel(first, x_ref, o_ref, sem):
    rows = o_ref.shape[0]
    copy = pltpu.make_async_copy(x_ref.at[pl.ds(first, rows), :], o_ref, sem)
    copy.start()
    copy.wait()


def take_rows(x, first, rows):
    return pl.pallas_call(
        functools.partial(take_kernel, first),
        in_specs=[pl.BlockSpec(memory_space=pltpu.VMEM)],
        out_specs=pl.BlockSpec(memory_space=pltpu.HBM),
        out_shape=jax.ShapeDtypeStruct((rows, x.shape[1]), x.dtype),
        scratch_shapes=[pltpu.SemaphoreType.DMA],
        compiler_params=pltpu.CompilerParams(vmem_limit_bytes=VMEM_SMALL),
        name="take_rows",
    )(x)


Y_OFFSETS = (0, 3, 1, 2)


def start_all(copies):
    for copy in copies:
        copy.start()


def wait_all(copies):
    for copy in copies:
        copy.wait()


def pack_kernel(queries, keys, values, *refs):
    outs, (both_s, query_s, sems, out_sems) = refs[:-4], refs[-4:]
    arrive, leave = [], []
    for j, distance in enumerate((0, 1, 3, 2)):
        first = lax.rem(lax.axis_index("y") + distance, 4) * WIDTH
        source = pl.ds(pl.multiple_of(first, WIDTH), WIDTH)
        pairs = (
            (keys.at[:, source], both_s.at[j, :, pl.ds(0, WIDTH)]),
            (values.at[:, source], both_s.at[j, :, pl.ds(WIDTH, WIDTH)]),
            (queries.at[:, source], query_s.at[j]),
        )
        for i, (src, dst) in enumerate(pairs):
            arrive.append(pltpu.make_async_copy(src, dst, sems.at[3 * j + i]))
        leave.append(pltpu.make_async_copy(both_s.at[j], outs[j], out_sems.at[j]))
        leave.append(pltpu.make_async_copy(query_s.at[j], outs[4 + j], out_sems.at[4 + j]))
    start_all(arrive)
    for j in range(4):
        wait_all(arrive[3 * j : 3 * j + 3])
        start_all(leave[2 * j : 2 * j + 2])
    wait_all(leave)


def pack_by_owner(queries, keys, values):
    shape = lambda width: jax.ShapeDtypeStruct((TOK, width), jnp.bfloat16)
    hbm = pl.BlockSpec(memory_space=pltpu.HBM)
    outs = pl.pallas_call(
        pack_kernel,
        in_specs=[hbm, hbm, hbm],
        out_specs=[hbm] * 8,
        out_shape=[shape(2 * WIDTH)] * 4 + [shape(WIDTH)] * 4,
        scratch_shapes=[
            pltpu.VMEM((4, TOK, 2 * WIDTH), jnp.bfloat16),
            pltpu.VMEM((4, TOK, WIDTH), jnp.bfloat16),
            pltpu.SemaphoreType.DMA((12,)),
            pltpu.SemaphoreType.DMA((8,)),
        ],
        compiler_params=pltpu.CompilerParams(vmem_limit_bytes=VMEM_GRANT),
        name="pack_by_owner",
    )(queries, keys, values)
    return outs[:4], outs[4:]


def stack_kernel(*refs):
    parts, out, sems = refs[:-2], refs[-2], refs[-1]
    rows = parts[0].shape[0]
    copies = [
        pltpu.make_async_copy(part, out.at[pl.ds(i * rows, rows), :], sems.at[i])
        for i, part in enumerate(parts)
    ]
    start_all(copies)
    wait_all(copies)


def stack(*parts, space=pltpu.HBM):
    rows, width = parts[0].shape
    return pl.pallas_call(
        stack_kernel,
        in_specs=[pl.BlockSpec(memory_space=pltpu.VMEM)] * len(parts),
        out_specs=pl.BlockSpec(memory_space=space),
        out_shape=jax.ShapeDtypeStruct((len(parts) * rows, width), parts[0].dtype),
        scratch_shapes=[pltpu.SemaphoreType.DMA((len(parts),))],
        compiler_params=pltpu.CompilerParams(vmem_limit_bytes=VMEM_SMALL),
        name="stack",
    )(*parts)


SEGMENTS = {
    2: ((0, 0, 160, 0, 0), (1, 0, 160, 1, 0), (1, 160, 160, 2, 0), (1, 320, 160, 3, 0)),
    3: (
        (0, 0, 160, 0, 0), (1, 0, 160, 1, 0), (1, 160, 80, 2, 0), (2, 0, 80, 2, 80),
        (2, 80, 160, 3, 0),
    ),
}


def lay_out(y, head, qs, pieces, q_s, k_s, v_s):
    keys = slice(head * HEAD_DIM, (head + 1) * HEAD_DIM)
    values = slice((HEADS + head) * HEAD_DIM, (HEADS + head + 1) * HEAD_DIM)
    for j, offset in enumerate(Y_OFFSETS):
        for r, q in enumerate(qs):
            first = (lax.rem(y + offset, 4) * len(qs) + r) * TOK
            place = pl.ds(pl.multiple_of(first, TOK), TOK)
            q_s[head, place, :] = q[j * TOK : (j + 1) * TOK, keys]
    for p, arrays in enumerate(pieces):
        for array, row, rows, j, start in SEGMENTS[len(arrays)]:
            group = lax.rem(y + Y_OFFSETS[j], 4)
            first = (group * len(pieces) + p) * TOK + start
            place = pl.ds(pl.multiple_of(first, 16), rows)
            k_s[head, place, :] = arrays[array][row : row + rows, keys]
            v_s[head, place, :] = arrays[array][row : row + rows, values]


def partial_attention(bias_ref, q_s, k_s, v_s, head):
    rows, keys_here = q_s.shape[1] // 4, k_s.shape[1]
    scores = []
    for yq in range(VIDEO_GROUPS):
        n = keys_here // 4 * (yq + 1)
        q = q_s[head, rows * yq : rows * (yq + 1), :]
        s = lax.dot_general(
            q, k_s[head, :n, :], (((1,), (1,)), ((), ())), preferred_element_type=jnp.float32
        )
        bias = [
            jnp.broadcast_to(bias_ref[r, yq : yq + 1, :n], (TOK, n)) for r in range(rows // TOK)
        ]
        scores.append(s + jnp.concatenate(bias, axis=0))
    tops = [jnp.max(s, axis=-1, keepdims=True) for s in scores]
    weights = [jnp.exp2((s - t) * FACTOR).astype(jnp.bfloat16) for s, t in zip(scores, tops)]
    ones = jnp.ones((keys_here, HEAD_DIM), jnp.bfloat16)
    values = jnp.concatenate([v_s[head], ones], axis=1)
    totals = [jnp.dot(w, values[: w.shape[1]], preferred_element_type=jnp.float32) for w in weights]
    return [
        (top * FACTOR, total[:, :HEAD_DIM], total[:, HEAD_DIM:]) for top, total in zip(tops, totals)
    ]


def merge_states(result, states):
    top, out, weight_sum = result
    both = functools.reduce(jnp.maximum, [log for _, log in states], top)
    factor = jnp.exp2(top - both)
    out, weight_sum = out * factor, weight_sum * factor
    for o, log in states:
        factor = jnp.exp2(log - both)
        out = out + o.astype(jnp.float32) * factor
        weight_sum = weight_sum + factor
    return both, out, weight_sum


def near_kernel(bias_ref, *refs):
    qs, refs, scratch = refs[:2], refs[2:-3], refs[-3:]
    pieces = [refs[2 * p : 2 * p + 2] for p in range(3)]
    o_here, log_here, o_there, log_there = refs[6:]
    place = lax.broadcasted_iota(jnp.int32, (TOK, HEAD_DIM), 1) // LOG_LANES
    for head in range(HEADS):
        columns = slice(head * HEAD_DIM, (head + 1) * HEAD_DIM)
        lay_out(lax.axis_index("y"), head, qs, pieces, *scratch)
        for yq, (top, out, weight_sum) in enumerate(partial_attention(bias_ref, *scratch, head)):
            out, log = out / weight_sum, top + jnp.log2(weight_sum)
            o_here[yq, :, columns], log_here[yq, :, columns] = out[:TOK], log[:TOK]
            o_there[yq, :, columns] = out[TOK:].astype(jnp.bfloat16)
            packed = log[TOK:]
            if head > 0:
                packed = jnp.where(place == head, packed, log_there[yq])
            log_there[yq] = packed


def far_kernel(bias_ref, q, *refs):
    parts, (o_in, log_in, o_out, log_out), scratch = refs[:3], refs[3:-3], refs[-3:]
    for head in range(HEADS):
        columns = slice(head * HEAD_DIM, (head + 1) * HEAD_DIM)
        lay_out(lax.axis_index("y"), head, (q,), (parts,), *scratch)
        for yq, result in enumerate(partial_attention(bias_ref, *scratch, head)):
            state = (o_in[yq, :, columns], log_in[yq, :, columns])
            top, out, weight_sum = merge_states(result, [state])
            o_out[yq, :, columns] = out / weight_sum
            log_out[yq, :, columns] = top + jnp.log2(weight_sum)


def last_kernel(bias_ref, q, *refs):
    parts, states, outs, scratch, o_s = refs[:3], refs[3:7], refs[7:11], refs[11:14], refs[14]
    o_here, log_here, o_there, log_there = states
    for head in range(HEADS):
        columns = slice(head * HEAD_DIM, (head + 1) * HEAD_DIM)
        lay_out(lax.axis_index("y"), head, (q,), (parts,), *scratch)
        for yq, result in enumerate(partial_attention(bias_ref, *scratch, head)):
            log = log_there[yq, :, head * LOG_LANES : head * LOG_LANES + 1]
            here = (o_here[yq, :, columns], log_here[yq, :, columns])
            there = (o_there[yq, :, columns], jnp.broadcast_to(log, (TOK, HEAD_DIM)))
            _, out, weight_sum = merge_states(result, [here, there])
            o_s[yq, :, columns] = (out / weight_sum).astype(jnp.bfloat16)
    for out, distance in zip(outs, (0, 1, 3, 2)):
        out[...] = o_s[lax.rem(lax.axis_index("y") + distance, 4)]


def attend(kernel, bias, qs, pieces, states, outs, scratch=()):
    vmem = pl.BlockSpec(memory_space=pltpu.VMEM)
    operands = [bias, *qs]
    for arrays in pieces:
        operands += arrays
    operands += states
    keys_here = 4 * TOK * len(pieces)
    return pl.pallas_call(
        kernel,
        in_specs=[vmem] * len(operands),
        out_specs=[vmem] * len(outs),
        out_shape=[jax.ShapeDtypeStruct(shape, dtype) for shape, dtype in outs],
        scratch_shapes=[
            pltpu.VMEM((HEADS, 4 * TOK * len(qs), HEAD_DIM), jnp.bfloat16),
            pltpu.VMEM((HEADS, keys_here, HEAD_DIM), jnp.bfloat16),
            pltpu.VMEM((HEADS, keys_here, HEAD_DIM), jnp.bfloat16),
            *scratch,
        ],
        compiler_params=pltpu.CompilerParams(vmem_limit_bytes=20 * 2**20),
        cost_estimate=pl.CostEstimate(
            flops=4 * 10**9 * len(pieces), bytes_accessed=2**20, transcendentals=0
        ),
        name=kernel.__name__,
    )(*operands)


def project_kernel(places, added, *refs):
    parts, w_ref, refs = refs[:4], refs[4], refs[5:]
    extra, outs, rows_s = refs[:added], refs[added:-1], refs[-1]
    for part, offset in zip(parts, Y_OFFSETS):
        first = lax.rem(lax.axis_index("y") + offset, 4) * WIDTH
        rows_s[:, pl.ds(pl.multiple_of(first, WIDTH), WIDTH)] = part[...]
    columns = w_ref.shape[1] // 8
    for i, (distance, half) in enumerate(places):
        first = (lax.rem(lax.axis_index("tp") + distance, 4) * 2 + half) * columns
        weights = w_ref[:, pl.ds(pl.multiple_of(first, columns), columns)]
        term = jnp.dot(rows_s[...], weights, preferred_element_type=jnp.float32)
        if added:
            term = term + extra[i][...].astype(jnp.float32)
        outs[i][...] = term.astype(outs[i].dtype)


def project(attended, out_weight, places, extra=(), dtype=jnp.bfloat16):
    depth, columns = out_weight.shape[0], out_weight.shape[1] // 8
    count = len(places)
    vmem = pl.BlockSpec(memory_space=pltpu.VMEM)
    return pl.pallas_call(
        functools.partial(project_kernel, places, len(extra)),
        in_specs=[vmem] * (5 + len(extra)),
        out_specs=[vmem] * count,
        out_shape=[jax.ShapeDtypeStruct((TOK, columns), dtype)] * count,
        scratch_shapes=[pltpu.VMEM((TOK, depth), jnp.bfloat16)],
        compiler_params=pltpu.CompilerParams(vmem_limit_bytes=VMEM_SMALL),
        cost_estimate=pl.CostEstimate(
            flops=2 * count * TOK * depth * columns,
            bytes_accessed=2 * count * depth * columns,
            transcendentals=0,
        ),
        name="project",
    )(*attended, out_weight, *extra)


def final_kernel(own_a, own_b, direct_a, direct_b, summed_a, summed_b, gate_ref, o_ref):
    columns = own_a.shape[1]
    for i, (own, direct, summed) in enumerate(
        ((own_a, direct_a, summed_a), (own_b, direct_b, summed_b))
    ):
        place = slice(i * columns, (i + 1) * columns)
        total = own[...] + direct[...].astype(jnp.float32) + summed[...].astype(jnp.float32)
        o_ref[:, place] = (total * gate_ref[:, place]).astype(o_ref.dtype)


def finish(halves, gate):
    rows, columns = halves[0].shape
    vmem = pl.BlockSpec(memory_space=pltpu.VMEM)
    return pl.pallas_call(
        final_kernel,
        in_specs=[vmem] * 7,
        out_specs=vmem,
        out_shape=jax.ShapeDtypeStruct((rows, 2 * columns), jnp.bfloat16),
        compiler_params=pltpu.CompilerParams(vmem_limit_bytes=VMEM_SMALL),
        name="finish",
    )(*halves, gate)


def shift(x, axis, step):
    size = lax.axis_size(axis)
    return lax.ppermute(x, axis, [(i, (i + step) % size) for i in range(size)])


def local(queries, keys, values, out_weight, gate_table, block_mask, levels):
    barrier = lax.optimization_barrier
    x, y, z, core = (lax.axis_index(name) for name in ("tp", "y", "z", "core"))

    visible = visible_matrix(block_mask).reshape(4, 4, 2, 4, 4, 2)
    seen = lax.dynamic_index_in_dim(visible, z, 1, keepdims=False)
    seen = jnp.stack(
        [lax.dynamic_index_in_dim(seen, (z + d) % 4, 3, keepdims=False) for d in (0, 3, 1, 2)],
        axis=3,
    )

    def bias_of(query_core, key_core, first, last):
        here = lax.dynamic_index_in_dim(seen, query_core, 1, keepdims=False)
        here = lax.dynamic_index_in_dim(here, key_core, 3, keepdims=False)[:, :, first:last]
        here = jnp.where(here, 0.0, masked_score).astype(jnp.float32)
        return jnp.repeat(here, TOK, axis=2).reshape(4, -1)

    biases = (
        jnp.stack([bias_of(core, core, 0, 3), bias_of(1 - core, core, 0, 3)]),
        bias_of(core, core, 3, 4)[None],
        bias_of(core, 1 - core, 3, 4)[None],
    )
    columns = gate_table.shape[1] // 4
    gate_part = lax.dynamic_slice(
        gate_table,
        (lax.dynamic_index_in_dim(levels, y, keepdims=False), x * columns),
        (1, columns),
    )

    (own, up, down, across), (q_own, q_up, q_down, q_across) = pack_by_owner(queries, keys, values)
    from_across = shift(across, "y", 2)
    from_down, from_up = shift(up, "y", 1), shift(down, "y", -1)
    own_before, own_after = shift(own, "z", 1), shift(own, "z", -1)
    own_far = shift(own_before, "z", 1)

    arrived = (from_down, from_up, from_across, q_up, q_down, q_across)
    arrived, own_before, own_after, own_far, biases, gate_part = barrier(
        (arrived, own_before, own_after, own_far, biases, gate_part)
    )
    from_down, from_up, from_across, q_up, q_down, q_across = arrived
    rest = stack(from_down, from_up, from_across)
    rest_before, rest_after = shift(rest, "z", 1), shift(rest, "z", -1)
    q_here = stack(q_own, shift(q_up, "y", 1), shift(q_down, "y", -1), shift(q_across, "y", 2))
    q_there = shift(q_here, "core", 1)
    own_near = stack(own, space=pltpu.VMEM)
    q_there, own_near, rest_before, rest_after = barrier(
        (q_there, own_near, rest_before, rest_after)
    )
    half = rest.shape[0] // 2
    far = (
        own_far,
        shift(take_rows(rest_before, 0, half), "z", 1),
        shift(take_rows(rest_after, half, half), "z", -1),
    )
    pieces = ((own_near, rest), (own_before, rest_before), (own_after, rest_after))
    f32, bf16 = jnp.float32, jnp.bfloat16
    state = (VIDEO_GROUPS, TOK, WIDTH)
    o_here, log_here, o_there, log_there = attend(
        near_kernel, biases[0], (q_here, q_there), pieces, (),
        [(state, f32), (state, f32), (state, bf16), ((VIDEO_GROUPS, TOK, HEAD_DIM), f32)],
    )
    o_here, far = barrier((o_here, far))
    far_there = tuple(shift(part, "core", 1) for part in far)
    here = attend(
        far_kernel, biases[1], (q_here,), (far,), (o_here, log_here),
        [(state, f32), (state, f32)],
    )
    there = (shift(o_there, "core", 1), shift(log_there, "core", 1))
    out, out_up, out_down, out_across = attend(
        last_kernel, biases[2], (q_here,), (far_there,), (*here, *there),
        [((TOK, WIDTH), bf16)] * 4, [pltpu.VMEM(state, bf16)],
    )
    attended = (out, shift(out_up, "y", 1), shift(out_down, "y", -1), shift(out_across, "y", 2))

    across_a, across_b = project(attended, out_weight, ((2, 0), (2, 1)))
    from_left, from_right = shift(across_a, "tp", 1), shift(across_b, "tp", -1)
    right_b, left_a = project(attended, out_weight, ((1, 1), (3, 0)))
    direct_b, direct_a = shift(right_b, "tp", 1), shift(left_a, "tp", -1)
    own_a, own_b = project(attended, out_weight, ((0, 0), (0, 1)), dtype=jnp.float32)
    right_a, left_b = project(
        attended, out_weight, ((1, 0), (3, 1)), (from_left, from_right)
    )
    summed_a, summed_b = shift(right_a, "tp", 1), shift(left_b, "tp", -1)
    return finish((own_a, own_b, direct_a, direct_b, summed_a, summed_b), gate_part)


def solution(mesh):
    fine = Mesh(mesh.devices.reshape(4, 4, 2, 4), ("y", "z", "core", "tp"))
    group = ("y", "z", "core")
    return jax.shard_map(
        local,
        mesh=fine,
        in_specs=(
            P(group, "tp"),
            P(group, "tp"),
            P(group, "tp"),
            P("tp", None),
            P(),
            P(),
            P(),
        ),
        out_specs=P(group, "tp"),
        check_vma=False,
    )
```

```python
import functools

import jax
import jax.numpy as jnp
from jax import lax
from jax.experimental import pallas as pl
from jax.experimental.pallas import tpu as pltpu
from jax.sharding import Mesh, PartitionSpec as P

HEAD_DIM = 128
VIDEO_GROUPS = 4
TOK = 160
HEADS = 3
WIDTH = HEADS * HEAD_DIM
FACTOR = HEAD_DIM ** -0.5 * 1.4426950408889634

masked_score = -1e30
VMEM_GRANT = 56 * 2**20
VMEM_SMALL = 8 * 2**20
LOG_LANES = 32


def visible_matrix(block_mask):
    blocks = block_mask.shape[0]
    block = jnp.arange(blocks, dtype=jnp.int32)
    per_group = blocks // VIDEO_GROUPS
    earlier = block[None, :] // per_group <= block[:, None] // per_group
    return (block[None, :] == block[:, None]) | ((block_mask == 1) & earlier)


def take_kernel(first, x_ref, o_ref, sem):
    rows = o_ref.shape[0]
    copy = pltpu.make_async_copy(x_ref.at[pl.ds(first, rows), :], o_ref, sem)
    copy.start()
    copy.wait()


def take_rows(x, first, rows):
    return pl.pallas_call(
        functools.partial(take_kernel, first),
        in_specs=[pl.BlockSpec(memory_space=pltpu.VMEM)],
        out_specs=pl.BlockSpec(memory_space=pltpu.HBM),
        out_shape=jax.ShapeDtypeStruct((rows, x.shape[1]), x.dtype),
        scratch_shapes=[pltpu.SemaphoreType.DMA],
        compiler_params=pltpu.CompilerParams(vmem_limit_bytes=VMEM_SMALL),
        name="take_rows",
    )(x)


Y_OFFSETS = (0, 3, 1, 2)


def start_all(copies):
    for copy in copies:
        copy.start()


def wait_all(copies):
    for copy in copies:
        copy.wait()


def pack_kernel(count, *refs):
    sources, outs, (stage_s, sems, out_sems) = refs[:count], refs[count:-3], refs[-3:]
    arrive, leave = [], []
    for j, distance in enumerate((0, 1, 3, 2)):
        first = lax.rem(lax.axis_index("y") + distance, 4) * WIDTH
        source = pl.ds(pl.multiple_of(first, WIDTH), WIDTH)
        for i, array in enumerate(sources):
            stage = stage_s.at[j, :, pl.ds(i * WIDTH, WIDTH)]
            arrive.append(pltpu.make_async_copy(array.at[:, source], stage, sems.at[j, i]))
        leave.append(pltpu.make_async_copy(stage_s.at[j], outs[j], out_sems.at[j]))
    start_all(arrive)
    for j in range(4):
        wait_all(arrive[count * j : count * (j + 1)])
        leave[j].start()
    wait_all(leave)


def pack_by_owner(*arrays):
    count = len(arrays)
    hbm = pl.BlockSpec(memory_space=pltpu.HBM)
    return pl.pallas_call(
        functools.partial(pack_kernel, count),
        in_specs=[hbm] * count,
        out_specs=[hbm] * 4,
        out_shape=[jax.ShapeDtypeStruct((TOK, count * WIDTH), jnp.bfloat16)] * 4,
        scratch_shapes=[
            pltpu.VMEM((4, TOK, count * WIDTH), jnp.bfloat16),
            pltpu.SemaphoreType.DMA((4, count)),
            pltpu.SemaphoreType.DMA((4,)),
        ],
        compiler_params=pltpu.CompilerParams(vmem_limit_bytes=VMEM_GRANT),
        name="pack_by_owner",
    )(*arrays)


def stack_kernel(*refs):
    parts, out, sems = refs[:-2], refs[-2], refs[-1]
    rows = parts[0].shape[0]
    copies = [
        pltpu.make_async_copy(part, out.at[pl.ds(i * rows, rows), :], sems.at[i])
        for i, part in enumerate(parts)
    ]
    start_all(copies)
    wait_all(copies)


def stack(*parts, space=pltpu.HBM):
    rows, width = parts[0].shape
    return pl.pallas_call(
        stack_kernel,
        in_specs=[pl.BlockSpec(memory_space=pltpu.VMEM)] * len(parts),
        out_specs=pl.BlockSpec(memory_space=space),
        out_shape=jax.ShapeDtypeStruct((len(parts) * rows, width), parts[0].dtype),
        scratch_shapes=[pltpu.SemaphoreType.DMA((len(parts),))],
        compiler_params=pltpu.CompilerParams(vmem_limit_bytes=VMEM_SMALL),
        name="stack",
    )(*parts)


SEGMENTS = {
    2: ((0, 0, 160, 0, 0), (1, 0, 160, 1, 0), (1, 160, 160, 2, 0), (1, 320, 160, 3, 0)),
    3: (
        (0, 0, 160, 0, 0), (1, 0, 160, 1, 0), (1, 160, 80, 2, 0), (2, 0, 80, 2, 80),
        (2, 80, 160, 3, 0),
    ),
}


def lay_out(y, head, qs, pieces, q_s, k_s, v_s):
    keys = slice(head * HEAD_DIM, (head + 1) * HEAD_DIM)
    values = slice((HEADS + head) * HEAD_DIM, (HEADS + head + 1) * HEAD_DIM)
    for j, offset in enumerate(Y_OFFSETS):
        for r, q in enumerate(qs):
            first = (lax.rem(y + offset, 4) * len(qs) + r) * TOK
            place = pl.ds(pl.multiple_of(first, TOK), TOK)
            q_s[head, place, :] = q[j * TOK : (j + 1) * TOK, keys]
    for p, arrays in enumerate(pieces):
        for array, row, rows, j, start in SEGMENTS[len(arrays)]:
            group = lax.rem(y + Y_OFFSETS[j], 4)
            first = (group * len(pieces) + p) * TOK + start
            place = pl.ds(pl.multiple_of(first, 16), rows)
            k_s[head, place, :] = arrays[array][row : row + rows, keys]
            v_s[head, place, :] = arrays[array][row : row + rows, values]


def partial_attention(bias_ref, q_s, k_s, v_s, head):
    rows, keys_here = q_s.shape[1] // 4, k_s.shape[1]
    scores = []
    for yq in range(VIDEO_GROUPS):
        n = keys_here // 4 * (yq + 1)
        q = q_s[head, rows * yq : rows * (yq + 1), :]
        s = lax.dot_general(
            q, k_s[head, :n, :], (((1,), (1,)), ((), ())), preferred_element_type=jnp.float32
        )
        bias = [
            jnp.broadcast_to(bias_ref[r, yq : yq + 1, :n], (TOK, n)) for r in range(rows // TOK)
        ]
        scores.append(s + jnp.concatenate(bias, axis=0))
    tops = [jnp.max(s, axis=-1, keepdims=True) for s in scores]
    weights = [jnp.exp2((s - t) * FACTOR).astype(jnp.bfloat16) for s, t in zip(scores, tops)]
    ones = jnp.ones((keys_here, HEAD_DIM), jnp.bfloat16)
    values = jnp.concatenate([v_s[head], ones], axis=1)
    totals = [jnp.dot(w, values[: w.shape[1]], preferred_element_type=jnp.float32) for w in weights]
    return [
        (top * FACTOR, total[:, :HEAD_DIM], total[:, HEAD_DIM:]) for top, total in zip(tops, totals)
    ]


def merge_states(result, states):
    top, out, weight_sum = result
    both = functools.reduce(jnp.maximum, [log for _, log in states], top)
    factor = jnp.exp2(top - both)
    out, weight_sum = out * factor, weight_sum * factor
    for o, log in states:
        factor = jnp.exp2(log - both)
        out = out + o.astype(jnp.float32) * factor
        weight_sum = weight_sum + factor
    return both, out, weight_sum


def near_kernel(bias_ref, *refs):
    qs, refs, scratch = refs[:2], refs[2:-3], refs[-3:]
    pieces = [refs[2 * p : 2 * p + 2] for p in range(3)]
    o_here, log_here, o_there, log_there = refs[6:]
    place = lax.broadcasted_iota(jnp.int32, (TOK, HEAD_DIM), 1) // LOG_LANES
    for head in range(HEADS):
        columns = slice(head * HEAD_DIM, (head + 1) * HEAD_DIM)
        lay_out(lax.axis_index("y"), head, qs, pieces, *scratch)
        for yq, (top, out, weight_sum) in enumerate(partial_attention(bias_ref, *scratch, head)):
            out, log = out / weight_sum, top + jnp.log2(weight_sum)
            o_here[yq, :, columns], log_here[yq, :, columns] = out[:TOK], log[:TOK]
            o_there[yq, :, columns] = out[TOK:].astype(jnp.bfloat16)
            packed = log[TOK:]
            if head > 0:
                packed = jnp.where(place == head, packed, log_there[yq])
            log_there[yq] = packed


def far_kernel(bias_ref, q, *refs):
    parts, (o_in, log_in, o_out, log_out), scratch = refs[:3], refs[3:-3], refs[-3:]
    for head in range(HEADS):
        columns = slice(head * HEAD_DIM, (head + 1) * HEAD_DIM)
        lay_out(lax.axis_index("y"), head, (q,), (parts,), *scratch)
        for yq, result in enumerate(partial_attention(bias_ref, *scratch, head)):
            state = (o_in[yq, :, columns], log_in[yq, :, columns])
            top, out, weight_sum = merge_states(result, [state])
            o_out[yq, :, columns] = out / weight_sum
            log_out[yq, :, columns] = top + jnp.log2(weight_sum)


def last_kernel(bias_ref, q, *refs):
    parts, states, outs, scratch, o_s = refs[:3], refs[3:7], refs[7:11], refs[11:14], refs[14]
    o_here, log_here, o_there, log_there = states
    for head in range(HEADS):
        columns = slice(head * HEAD_DIM, (head + 1) * HEAD_DIM)
        lay_out(lax.axis_index("y"), head, (q,), (parts,), *scratch)
        for yq, result in enumerate(partial_attention(bias_ref, *scratch, head)):
            log = log_there[yq, :, head * LOG_LANES : head * LOG_LANES + 1]
            here = (o_here[yq, :, columns], log_here[yq, :, columns])
            there = (o_there[yq, :, columns], jnp.broadcast_to(log, (TOK, HEAD_DIM)))
            _, out, weight_sum = merge_states(result, [here, there])
            o_s[yq, :, columns] = (out / weight_sum).astype(jnp.bfloat16)
    for out, distance in zip(outs, (0, 1, 3, 2)):
        out[...] = o_s[lax.rem(lax.axis_index("y") + distance, 4)]


def attend(kernel, bias, qs, pieces, states, outs, scratch=()):
    vmem = pl.BlockSpec(memory_space=pltpu.VMEM)
    operands = [bias, *qs]
    for arrays in pieces:
        operands += arrays
    operands += states
    keys_here = 4 * TOK * len(pieces)
    return pl.pallas_call(
        kernel,
        in_specs=[vmem] * len(operands),
        out_specs=[vmem] * len(outs),
        out_shape=[jax.ShapeDtypeStruct(shape, dtype) for shape, dtype in outs],
        scratch_shapes=[
            pltpu.VMEM((HEADS, 4 * TOK * len(qs), HEAD_DIM), jnp.bfloat16),
            pltpu.VMEM((HEADS, keys_here, HEAD_DIM), jnp.bfloat16),
            pltpu.VMEM((HEADS, keys_here, HEAD_DIM), jnp.bfloat16),
            *scratch,
        ],
        compiler_params=pltpu.CompilerParams(vmem_limit_bytes=20 * 2**20),
        cost_estimate=pl.CostEstimate(
            flops=4 * 10**9 * len(pieces), bytes_accessed=2**20, transcendentals=0
        ),
        name=kernel.__name__,
    )(*operands)


def project_kernel(places, *refs):
    parts, w_ref, outs, rows_s = refs[:4], refs[4], refs[5:-1], refs[-1]
    for part, offset in zip(parts, Y_OFFSETS):
        first = lax.rem(lax.axis_index("y") + offset, 4) * WIDTH
        rows_s[:, pl.ds(pl.multiple_of(first, WIDTH), WIDTH)] = part[...]
    columns = w_ref.shape[1] // 8
    for i, (distance, half) in enumerate(places):
        first = (lax.rem(lax.axis_index("tp") + distance, 4) * 2 + half) * columns
        weights = w_ref[:, pl.ds(pl.multiple_of(first, columns), columns)]
        term = jnp.dot(rows_s[...], weights, preferred_element_type=jnp.float32)
        outs[i][...] = term.astype(outs[i].dtype)


def project(attended, out_weight, places, dtype=jnp.bfloat16):
    depth, columns = out_weight.shape[0], out_weight.shape[1] // 8
    count = len(places)
    vmem = pl.BlockSpec(memory_space=pltpu.VMEM)
    return pl.pallas_call(
        functools.partial(project_kernel, places),
        in_specs=[vmem] * 5,
        out_specs=[vmem] * count,
        out_shape=[jax.ShapeDtypeStruct((TOK, columns), dtype)] * count,
        scratch_shapes=[pltpu.VMEM((TOK, depth), jnp.bfloat16)],
        compiler_params=pltpu.CompilerParams(vmem_limit_bytes=VMEM_SMALL),
        cost_estimate=pl.CostEstimate(
            flops=2 * count * TOK * depth * columns,
            bytes_accessed=2 * count * depth * columns,
            transcendentals=0,
        ),
        name="project",
    )(*attended, out_weight)


def add_kernel(*refs):
    count = len(refs) // 3
    for i in range(count):
        total = refs[i][...] + refs[count + i][...].astype(jnp.float32)
        refs[2 * count + i][...] = total.astype(refs[2 * count + i].dtype)


def add(terms, arrived, dtype):
    vmem = pl.BlockSpec(memory_space=pltpu.VMEM)
    return pl.pallas_call(
        add_kernel,
        in_specs=[vmem] * 4,
        out_specs=[vmem] * 2,
        out_shape=[jax.ShapeDtypeStruct(terms[0].shape, dtype)] * 2,
        compiler_params=pltpu.CompilerParams(vmem_limit_bytes=VMEM_SMALL),
        name="add",
    )(*terms, *arrived)


def final_kernel(own_a, own_b, summed_a, summed_b, gate_ref, o_ref):
    columns = own_a.shape[1]
    for i, (own, summed) in enumerate(((own_a, summed_a), (own_b, summed_b))):
        place = slice(i * columns, (i + 1) * columns)
        total = own[...] + summed[...].astype(jnp.float32)
        o_ref[:, place] = (total * gate_ref[:, place]).astype(o_ref.dtype)


def finish(halves, gate):
    rows, columns = halves[0].shape
    vmem = pl.BlockSpec(memory_space=pltpu.VMEM)
    return pl.pallas_call(
        final_kernel,
        in_specs=[vmem] * 5,
        out_specs=vmem,
        out_shape=jax.ShapeDtypeStruct((rows, 2 * columns), jnp.bfloat16),
        compiler_params=pltpu.CompilerParams(vmem_limit_bytes=VMEM_SMALL),
        name="finish",
    )(*halves, gate)


def shift(x, axis, step):
    size = lax.axis_size(axis)
    return lax.ppermute(x, axis, [(i, (i + step) % size) for i in range(size)])


def local(queries, keys, values, out_weight, gate_table, block_mask, levels):
    barrier = lax.optimization_barrier
    x, y, z, core = (lax.axis_index(name) for name in ("tp", "y", "z", "core"))

    visible = visible_matrix(block_mask).reshape(4, 4, 2, 4, 4, 2)
    seen = lax.dynamic_index_in_dim(visible, z, 1, keepdims=False)
    seen = jnp.stack(
        [lax.dynamic_index_in_dim(seen, (z + d) % 4, 3, keepdims=False) for d in (0, 3, 1, 2)],
        axis=3,
    )

    def bias_of(query_core, key_core, first, last):
        here = lax.dynamic_index_in_dim(seen, query_core, 1, keepdims=False)
        here = lax.dynamic_index_in_dim(here, key_core, 3, keepdims=False)[:, :, first:last]
        here = jnp.where(here, 0.0, masked_score).astype(jnp.float32)
        return jnp.repeat(here, TOK, axis=2).reshape(4, -1)

    biases = (
        jnp.stack([bias_of(core, core, 0, 3), bias_of(1 - core, core, 0, 3)]),
        bias_of(core, core, 3, 4)[None],
        bias_of(core, 1 - core, 3, 4)[None],
    )
    columns = gate_table.shape[1] // 4
    gate_part = lax.dynamic_slice(
        gate_table,
        (lax.dynamic_index_in_dim(levels, y, keepdims=False), x * columns),
        (1, columns),
    )

    own, up, down, across = pack_by_owner(keys, values)
    q_own, q_up, q_down, q_across = pack_by_owner(queries)
    from_across = shift(across, "y", 2)
    from_down, from_up = shift(up, "y", 1), shift(down, "y", -1)
    own_before, own_after = shift(own, "z", 1), shift(own, "z", -1)
    own_far = shift(own_before, "z", 1)

    arrived = (from_down, from_up, from_across, q_up, q_down, q_across)
    arrived, own_before, own_after, own_far, biases, gate_part = barrier(
        (arrived, own_before, own_after, own_far, biases, gate_part)
    )
    from_down, from_up, from_across, q_up, q_down, q_across = arrived
    rest = stack(from_down, from_up, from_across)
    rest_before, rest_after = shift(rest, "z", 1), shift(rest, "z", -1)
    q_here = stack(q_own, shift(q_up, "y", 1), shift(q_down, "y", -1), shift(q_across, "y", 2))
    q_there = shift(q_here, "core", 1)
    own_near = stack(own, space=pltpu.VMEM)
    q_there, own_near, rest_before, rest_after = barrier(
        (q_there, own_near, rest_before, rest_after)
    )
    half = rest.shape[0] // 2
    far = (
        own_far,
        shift(take_rows(rest_before, 0, half), "z", 1),
        shift(take_rows(rest_after, half, half), "z", -1),
    )
    pieces = ((own_near, rest), (own_before, rest_before), (own_after, rest_after))
    f32, bf16 = jnp.float32, jnp.bfloat16
    state = (VIDEO_GROUPS, TOK, WIDTH)
    o_here, log_here, o_there, log_there = attend(
        near_kernel, biases[0], (q_here, q_there), pieces, (),
        [(state, f32), (state, f32), (state, bf16), ((VIDEO_GROUPS, TOK, HEAD_DIM), f32)],
    )
    o_here, far = barrier((o_here, far))
    far_there = tuple(shift(part, "core", 1) for part in far)
    here = attend(
        far_kernel, biases[1], (q_here,), (far,), (o_here, log_here),
        [(state, f32), (state, f32)],
    )
    there = (shift(o_there, "core", 1), shift(log_there, "core", 1))
    out, out_up, out_down, out_across = attend(
        last_kernel, biases[2], (q_here,), (far_there,), (*here, *there),
        [((TOK, WIDTH), bf16)] * 4, [pltpu.VMEM(state, bf16)],
    )
    attended = (out, shift(out_up, "y", 1), shift(out_down, "y", -1), shift(out_across, "y", 2))

    across_a, across_b = project(attended, out_weight, ((2, 0), (2, 1)))
    from_left, from_right = shift(across_a, "tp", 1), shift(across_b, "tp", -1)
    right_b, left_a = project(attended, out_weight, ((1, 1), (3, 0)))
    direct_b, direct_a = shift(right_b, "tp", 1), shift(left_a, "tp", -1)
    right_a, left_b, own_a, own_b = project(
        attended, out_weight, ((1, 0), (3, 1), (0, 0), (0, 1)), dtype=f32
    )
    right_a, left_b = add((right_a, left_b), (from_left, from_right), bf16)
    summed_a, summed_b = shift(right_a, "tp", 1), shift(left_b, "tp", -1)
    own_a, own_b = add((own_a, own_b), (direct_a, direct_b), f32)
    return finish((own_a, own_b, summed_a, summed_b), gate_part)


def solution(mesh):
    fine = Mesh(mesh.devices.reshape(4, 4, 2, 4), ("y", "z", "core", "tp"))
    group = ("y", "z", "core")
    return jax.shard_map(
        local,
        mesh=fine,
        in_specs=(
            P(group, "tp"),
            P(group, "tp"),
            P(group, "tp"),
            P("tp", None),
            P(),
            P(),
            P(),
        ),
        out_specs=P(group, "tp"),
        check_vma=False,
    )
```

```python
import functools

import jax
import jax.numpy as jnp
from jax import lax
from jax.experimental import pallas as pl
from jax.experimental.pallas import tpu as pltpu
from jax.sharding import Mesh, PartitionSpec as P

HEAD_DIM = 128
VIDEO_GROUPS = 4
TOK = 160
HEADS = 3
WIDTH = HEADS * HEAD_DIM
FACTOR = HEAD_DIM ** -0.5 * 1.4426950408889634

masked_score = -1e30
VMEM_GRANT = 56 * 2**20
VMEM_SMALL = 8 * 2**20
LOG_LANES = 32


def visible_matrix(block_mask):
    blocks = block_mask.shape[0]
    block = jnp.arange(blocks, dtype=jnp.int32)
    per_group = blocks // VIDEO_GROUPS
    earlier = block[None, :] // per_group <= block[:, None] // per_group
    return (block[None, :] == block[:, None]) | ((block_mask == 1) & earlier)


def take_kernel(first, x_ref, o_ref, sem):
    rows = o_ref.shape[0]
    copy = pltpu.make_async_copy(x_ref.at[pl.ds(first, rows), :], o_ref, sem)
    copy.start()
    copy.wait()


def take_rows(x, first, rows):
    return pl.pallas_call(
        functools.partial(take_kernel, first),
        in_specs=[pl.BlockSpec(memory_space=pltpu.VMEM)],
        out_specs=pl.BlockSpec(memory_space=pltpu.HBM),
        out_shape=jax.ShapeDtypeStruct((rows, x.shape[1]), x.dtype),
        scratch_shapes=[pltpu.SemaphoreType.DMA],
        compiler_params=pltpu.CompilerParams(vmem_limit_bytes=VMEM_SMALL),
        name="take_rows",
    )(x)


Y_OFFSETS = (0, 3, 1, 2)


def start_all(copies):
    for copy in copies:
        copy.start()


def wait_all(copies):
    for copy in copies:
        copy.wait()


def pack_kernel(count, *refs):
    sources, outs, (stage_s, sems, out_sems) = refs[:count], refs[count:-3], refs[-3:]
    arrive, leave = [], []
    for j, distance in enumerate((0, 1, 3, 2)):
        first = lax.rem(lax.axis_index("y") + distance, 4) * WIDTH
        source = pl.ds(pl.multiple_of(first, WIDTH), WIDTH)
        for i, array in enumerate(sources):
            stage = stage_s.at[j, :, pl.ds(i * WIDTH, WIDTH)]
            arrive.append(pltpu.make_async_copy(array.at[:, source], stage, sems.at[j, i]))
        leave.append(pltpu.make_async_copy(stage_s.at[j], outs[j], out_sems.at[j]))
    start_all(arrive)
    for j in range(4):
        wait_all(arrive[count * j : count * (j + 1)])
        leave[j].start()
    wait_all(leave)


def pack_by_owner(*arrays):
    count = len(arrays)
    hbm = pl.BlockSpec(memory_space=pltpu.HBM)
    return pl.pallas_call(
        functools.partial(pack_kernel, count),
        in_specs=[hbm] * count,
        out_specs=[hbm] * 4,
        out_shape=[jax.ShapeDtypeStruct((TOK, count * WIDTH), jnp.bfloat16)] * 4,
        scratch_shapes=[
            pltpu.VMEM((4, TOK, count * WIDTH), jnp.bfloat16),
            pltpu.SemaphoreType.DMA((4, count)),
            pltpu.SemaphoreType.DMA((4,)),
        ],
        compiler_params=pltpu.CompilerParams(vmem_limit_bytes=VMEM_GRANT),
        name="pack_by_owner",
    )(*arrays)


def stack_kernel(*refs):
    parts, out, sems = refs[:-2], refs[-2], refs[-1]
    rows = parts[0].shape[0]
    copies = [
        pltpu.make_async_copy(part, out.at[pl.ds(i * rows, rows), :], sems.at[i])
        for i, part in enumerate(parts)
    ]
    start_all(copies)
    wait_all(copies)


def stack(*parts, space=pltpu.HBM):
    rows, width = parts[0].shape
    return pl.pallas_call(
        stack_kernel,
        in_specs=[pl.BlockSpec(memory_space=pltpu.VMEM)] * len(parts),
        out_specs=pl.BlockSpec(memory_space=space),
        out_shape=jax.ShapeDtypeStruct((len(parts) * rows, width), parts[0].dtype),
        scratch_shapes=[pltpu.SemaphoreType.DMA((len(parts),))],
        compiler_params=pltpu.CompilerParams(vmem_limit_bytes=VMEM_SMALL),
        name="stack",
    )(*parts)


SEGMENTS = {
    2: ((0, 0, 160, 0, 0), (1, 0, 160, 1, 0), (1, 160, 160, 2, 0), (1, 320, 160, 3, 0)),
    3: (
        (0, 0, 160, 0, 0), (1, 0, 160, 1, 0), (1, 160, 80, 2, 0), (2, 0, 80, 2, 80),
        (2, 80, 160, 3, 0),
    ),
}


def lay_out(y, head, qs, pieces, q_s, k_s, v_s):
    keys = slice(head * HEAD_DIM, (head + 1) * HEAD_DIM)
    values = slice((HEADS + head) * HEAD_DIM, (HEADS + head + 1) * HEAD_DIM)
    for j, offset in enumerate(Y_OFFSETS):
        for r, q in enumerate(qs):
            first = (lax.rem(y + offset, 4) * len(qs) + r) * TOK
            place = pl.ds(pl.multiple_of(first, TOK), TOK)
            q_s[head, place, :] = q[j * TOK : (j + 1) * TOK, keys]
    for p, arrays in enumerate(pieces):
        for array, row, rows, j, start in SEGMENTS[len(arrays)]:
            group = lax.rem(y + Y_OFFSETS[j], 4)
            first = (group * len(pieces) + p) * TOK + start
            place = pl.ds(pl.multiple_of(first, 16), rows)
            k_s[head, place, :] = arrays[array][row : row + rows, keys]
            v_s[head, place, :] = arrays[array][row : row + rows, values]


def partial_attention(bias_ref, q_s, k_s, v_s, head):
    rows, keys_here = q_s.shape[1] // 4, k_s.shape[1]
    scores = []
    for yq in range(VIDEO_GROUPS):
        n = keys_here // 4 * (yq + 1)
        q = q_s[head, rows * yq : rows * (yq + 1), :]
        s = lax.dot_general(
            q, k_s[head, :n, :], (((1,), (1,)), ((), ())), preferred_element_type=jnp.float32
        )
        bias = [
            jnp.broadcast_to(bias_ref[r, yq : yq + 1, :n], (TOK, n)) for r in range(rows // TOK)
        ]
        scores.append(s + jnp.concatenate(bias, axis=0))
    tops = [jnp.max(s, axis=-1, keepdims=True) for s in scores]
    weights = [jnp.exp2((s - t) * FACTOR).astype(jnp.bfloat16) for s, t in zip(scores, tops)]
    ones = jnp.ones((keys_here, HEAD_DIM), jnp.bfloat16)
    values = jnp.concatenate([v_s[head], ones], axis=1)
    totals = [jnp.dot(w, values[: w.shape[1]], preferred_element_type=jnp.float32) for w in weights]
    return [
        (top * FACTOR, total[:, :HEAD_DIM], total[:, HEAD_DIM:]) for top, total in zip(tops, totals)
    ]


def merge_states(result, states):
    top, out, weight_sum = result
    both = functools.reduce(jnp.maximum, [log for _, log in states], top)
    factor = jnp.exp2(top - both)
    out, weight_sum = out * factor, weight_sum * factor
    for o, log in states:
        factor = jnp.exp2(log - both)
        out = out + o.astype(jnp.float32) * factor
        weight_sum = weight_sum + factor
    return both, out, weight_sum


def near_kernel(bias_ref, *refs):
    qs, refs, scratch = refs[:2], refs[2:-3], refs[-3:]
    pieces = [refs[2 * p : 2 * p + 2] for p in range(3)]
    o_here, log_here, o_there, log_there = refs[6:]
    place = lax.broadcasted_iota(jnp.int32, (TOK, HEAD_DIM), 1) // LOG_LANES
    for head in range(HEADS):
        columns = slice(head * HEAD_DIM, (head + 1) * HEAD_DIM)
        lay_out(lax.axis_index("y"), head, qs, pieces, *scratch)
        for yq, (top, out, weight_sum) in enumerate(partial_attention(bias_ref, *scratch, head)):
            out, log = out / weight_sum, top + jnp.log2(weight_sum)
            o_here[yq, :, columns], log_here[yq, :, columns] = out[:TOK], log[:TOK]
            o_there[yq, :, columns] = out[TOK:].astype(jnp.bfloat16)
            packed = log[TOK:]
            if head > 0:
                packed = jnp.where(place == head, packed, log_there[yq])
            log_there[yq] = packed


def far_kernel(bias_ref, q, *refs):
    parts, (o_in, log_in, o_out, log_out), scratch = refs[:3], refs[3:-3], refs[-3:]
    for head in range(HEADS):
        columns = slice(head * HEAD_DIM, (head + 1) * HEAD_DIM)
        lay_out(lax.axis_index("y"), head, (q,), (parts,), *scratch)
        for yq, result in enumerate(partial_attention(bias_ref, *scratch, head)):
            state = (o_in[yq, :, columns], log_in[yq, :, columns])
            top, out, weight_sum = merge_states(result, [state])
            o_out[yq, :, columns] = out / weight_sum
            log_out[yq, :, columns] = top + jnp.log2(weight_sum)


def last_kernel(targets, bias_ref, q, *refs):
    parts, states, outs, scratch = refs[:3], refs[3:7], refs[7:-3], refs[-3:]
    o_here, log_here, o_there, log_there = states
    k_s, v_s = scratch[1:]
    ones = jnp.ones((k_s.shape[1], HEAD_DIM), jnp.bfloat16)
    for head in range(HEADS):
        columns = slice(head * HEAD_DIM, (head + 1) * HEAD_DIM)
        lay_out(lax.axis_index("y"), head, (), (parts,), *scratch)
    groups = [lax.rem(lax.axis_index("y") + Y_OFFSETS[j], 4) for j in targets]
    for head in range(HEADS):
        columns = slice(head * HEAD_DIM, (head + 1) * HEAD_DIM)
        scores = [
            lax.dot_general(
                q[j * TOK : (j + 1) * TOK, columns], k_s[head], (((1,), (1,)), ((), ())),
                preferred_element_type=jnp.float32,
            ) + bias_ref[0, pl.ds(group, 1), :]
            for j, group in zip(targets, groups)
        ]
        tops = [jnp.max(s, axis=-1, keepdims=True) for s in scores]
        weights = [jnp.exp2((s - t) * FACTOR).astype(jnp.bfloat16) for s, t in zip(scores, tops)]
        values = jnp.concatenate([v_s[head], ones], axis=1)
        for group, top, w, out_ref in zip(groups, tops, weights, outs):
            total = jnp.dot(w, values, preferred_element_type=jnp.float32)
            log = log_there[group, :, head * LOG_LANES : head * LOG_LANES + 1]
            here = (o_here[group, :, columns], log_here[group, :, columns])
            there = (o_there[group, :, columns], jnp.broadcast_to(log, (TOK, HEAD_DIM)))
            result = (top * FACTOR, total[:, :HEAD_DIM], total[:, HEAD_DIM:])
            _, out, weight_sum = merge_states(result, [here, there])
            out_ref[:, columns] = (out / weight_sum).astype(jnp.bfloat16)


def attend(kernel, bias, qs, pieces, states, outs, name):
    vmem = pl.BlockSpec(memory_space=pltpu.VMEM)
    operands = [bias, *qs]
    for arrays in pieces:
        operands += arrays
    operands += states
    keys_here = 4 * TOK * len(pieces)
    return pl.pallas_call(
        kernel,
        in_specs=[vmem] * len(operands),
        out_specs=[vmem] * len(outs),
        out_shape=[jax.ShapeDtypeStruct(shape, dtype) for shape, dtype in outs],
        scratch_shapes=[
            pltpu.VMEM((HEADS, 4 * TOK * len(qs), HEAD_DIM), jnp.bfloat16),
            pltpu.VMEM((HEADS, keys_here, HEAD_DIM), jnp.bfloat16),
            pltpu.VMEM((HEADS, keys_here, HEAD_DIM), jnp.bfloat16),
        ],
        compiler_params=pltpu.CompilerParams(vmem_limit_bytes=20 * 2**20),
        cost_estimate=pl.CostEstimate(
            flops=4 * 10**9 * len(pieces), bytes_accessed=2**20, transcendentals=0
        ),
        name=name,
    )(*operands)


def project_kernel(places, *refs):
    parts, w_ref, outs, rows_s = refs[:4], refs[4], refs[5:-1], refs[-1]
    for part, offset in zip(parts, Y_OFFSETS):
        first = lax.rem(lax.axis_index("y") + offset, 4) * WIDTH
        rows_s[:, pl.ds(pl.multiple_of(first, WIDTH), WIDTH)] = part[...]
    columns = w_ref.shape[1] // 8
    for i, (distance, half) in enumerate(places):
        first = (lax.rem(lax.axis_index("tp") + distance, 4) * 2 + half) * columns
        weights = w_ref[:, pl.ds(pl.multiple_of(first, columns), columns)]
        term = jnp.dot(rows_s[...], weights, preferred_element_type=jnp.float32)
        outs[i][...] = term.astype(outs[i].dtype)


def project(attended, out_weight, places, dtype=jnp.bfloat16):
    depth, columns = out_weight.shape[0], out_weight.shape[1] // 8
    count = len(places)
    vmem = pl.BlockSpec(memory_space=pltpu.VMEM)
    return pl.pallas_call(
        functools.partial(project_kernel, places),
        in_specs=[vmem] * 5,
        out_specs=[vmem] * count,
        out_shape=[jax.ShapeDtypeStruct((TOK, columns), dtype)] * count,
        scratch_shapes=[pltpu.VMEM((TOK, depth), jnp.bfloat16)],
        compiler_params=pltpu.CompilerParams(vmem_limit_bytes=VMEM_SMALL),
        cost_estimate=pl.CostEstimate(
            flops=2 * count * TOK * depth * columns,
            bytes_accessed=2 * count * depth * columns,
            transcendentals=0,
        ),
        name="project",
    )(*attended, out_weight)


def add_kernel(*refs):
    count = len(refs) // 3
    for i in range(count):
        total = refs[i][...] + refs[count + i][...].astype(jnp.float32)
        refs[2 * count + i][...] = total.astype(refs[2 * count + i].dtype)


def add(terms, arrived, dtype):
    vmem = pl.BlockSpec(memory_space=pltpu.VMEM)
    return pl.pallas_call(
        add_kernel,
        in_specs=[vmem] * 4,
        out_specs=[vmem] * 2,
        out_shape=[jax.ShapeDtypeStruct(terms[0].shape, dtype)] * 2,
        compiler_params=pltpu.CompilerParams(vmem_limit_bytes=VMEM_SMALL),
        name="add",
    )(*terms, *arrived)


def final_kernel(own_a, own_b, summed_a, summed_b, gate_ref, o_ref):
    columns = own_a.shape[1]
    for i, (own, summed) in enumerate(((own_a, summed_a), (own_b, summed_b))):
        place = slice(i * columns, (i + 1) * columns)
        total = own[...] + summed[...].astype(jnp.float32)
        o_ref[:, place] = (total * gate_ref[:, place]).astype(o_ref.dtype)


def finish(halves, gate):
    rows, columns = halves[0].shape
    vmem = pl.BlockSpec(memory_space=pltpu.VMEM)
    return pl.pallas_call(
        final_kernel,
        in_specs=[vmem] * 5,
        out_specs=vmem,
        out_shape=jax.ShapeDtypeStruct((rows, 2 * columns), jnp.bfloat16),
        compiler_params=pltpu.CompilerParams(vmem_limit_bytes=VMEM_SMALL),
        name="finish",
    )(*halves, gate)


def shift(x, axis, step):
    size = lax.axis_size(axis)
    return lax.ppermute(x, axis, [(i, (i + step) % size) for i in range(size)])


def local(queries, keys, values, out_weight, gate_table, block_mask, levels):
    barrier = lax.optimization_barrier
    x, y, z, core = (lax.axis_index(name) for name in ("tp", "y", "z", "core"))

    visible = visible_matrix(block_mask).reshape(4, 4, 2, 4, 4, 2)
    seen = lax.dynamic_index_in_dim(visible, z, 1, keepdims=False)
    seen = jnp.stack(
        [lax.dynamic_index_in_dim(seen, (z + d) % 4, 3, keepdims=False) for d in (0, 3, 1, 2)],
        axis=3,
    )

    def bias_of(query_core, key_core, first, last):
        here = lax.dynamic_index_in_dim(seen, query_core, 1, keepdims=False)
        here = lax.dynamic_index_in_dim(here, key_core, 3, keepdims=False)[:, :, first:last]
        here = jnp.where(here, 0.0, masked_score).astype(jnp.float32)
        return jnp.repeat(here, TOK, axis=2).reshape(4, -1)

    biases = (
        jnp.stack([bias_of(core, core, 0, 3), bias_of(1 - core, core, 0, 3)]),
        bias_of(core, core, 3, 4)[None],
        bias_of(core, 1 - core, 3, 4)[None],
    )
    columns = gate_table.shape[1] // 4
    gate_part = lax.dynamic_slice(
        gate_table,
        (lax.dynamic_index_in_dim(levels, y, keepdims=False), x * columns),
        (1, columns),
    )

    own, up, down, across = pack_by_owner(keys, values)
    q_own, q_up, q_down, q_across = pack_by_owner(queries)
    from_across = shift(across, "y", 2)
    from_down, from_up = shift(up, "y", 1), shift(down, "y", -1)
    own_before, own_after = shift(own, "z", 1), shift(own, "z", -1)
    own_far = shift(own_before, "z", 1)

    arrived = (from_down, from_up, from_across, q_up, q_down, q_across)
    arrived, own_before, own_after, own_far, biases, gate_part = barrier(
        (arrived, own_before, own_after, own_far, biases, gate_part)
    )
    from_down, from_up, from_across, q_up, q_down, q_across = arrived
    rest = stack(from_down, from_up, from_across)
    rest_before, rest_after = shift(rest, "z", 1), shift(rest, "z", -1)
    q_here = stack(q_own, shift(q_up, "y", 1), shift(q_down, "y", -1), shift(q_across, "y", 2))
    q_there = shift(q_here, "core", 1)
    own_near = stack(own, space=pltpu.VMEM)
    q_there, own_near, rest_before, rest_after = barrier(
        (q_there, own_near, rest_before, rest_after)
    )
    half = rest.shape[0] // 2
    far = (
        own_far,
        shift(take_rows(rest_before, 0, half), "z", 1),
        shift(take_rows(rest_after, half, half), "z", -1),
    )
    pieces = ((own_near, rest), (own_before, rest_before), (own_after, rest_after))
    f32, bf16 = jnp.float32, jnp.bfloat16
    state = (VIDEO_GROUPS, TOK, WIDTH)
    o_here, log_here, o_there, log_there = attend(
        near_kernel, biases[0], (q_here, q_there), pieces, (),
        [(state, f32), (state, f32), (state, bf16), ((VIDEO_GROUPS, TOK, HEAD_DIM), f32)],
        "attend_near",
    )
    o_here, far = barrier((o_here, far))
    far_there = tuple(shift(part, "core", 1) for part in far)
    here = attend(
        far_kernel, biases[1], (q_here,), (far,), (o_here, log_here),
        [(state, f32), (state, f32)], "attend_far",
    )
    there = (shift(o_there, "core", 1), shift(log_there, "core", 1))

    def last(*targets):
        return attend(
            functools.partial(last_kernel, targets), biases[2], (q_here,), (far_there,),
            (*here, *there), [((TOK, WIDTH), bf16)] * len(targets), "attend_last",
        )

    (out_across,) = last(3)
    out_down, out_up = last(1, 2)
    (out,) = last(0)
    attended = (out, shift(out_up, "y", 1), shift(out_down, "y", -1), shift(out_across, "y", 2))

    across_a, across_b = project(attended, out_weight, ((2, 0), (2, 1)))
    from_left, from_right = shift(across_a, "tp", 1), shift(across_b, "tp", -1)
    right_b, left_a = project(attended, out_weight, ((1, 1), (3, 0)))
    direct_b, direct_a = shift(right_b, "tp", 1), shift(left_a, "tp", -1)
    right_a, left_b, own_a, own_b = project(
        attended, out_weight, ((1, 0), (3, 1), (0, 0), (0, 1)), dtype=f32
    )
    right_a, left_b = add((right_a, left_b), (from_left, from_right), bf16)
    summed_a, summed_b = shift(right_a, "tp", 1), shift(left_b, "tp", -1)
    own_a, own_b = add((own_a, own_b), (direct_a, direct_b), f32)
    return finish((own_a, own_b, summed_a, summed_b), gate_part)


def solution(mesh):
    fine = Mesh(mesh.devices.reshape(4, 4, 2, 4), ("y", "z", "core", "tp"))
    group = ("y", "z", "core")
    return jax.shard_map(
        local,
        mesh=fine,
        in_specs=(
            P(group, "tp"),
            P(group, "tp"),
            P(group, "tp"),
            P("tp", None),
            P(),
            P(),
            P(),
        ),
        out_specs=P(group, "tp"),
        check_vma=False,
    )
```
